32 devices in a mesh: sector: 4 (over y, core), axial: 8 (over z, x).
Axes of the slice: x: 2, y: 2, z: 4, core: 2. Of those that a mesh axis runs over, the one named last changes fastest.
Arguments:
- adjoint: float32 [5, 64, 32768], P(None, None, ('sector', 'axial')), may hold values from -6 to 6
- velocity: bfloat16 [3, 64, 32768], P(None, None, ('sector', 'axial')), may hold values from -6 to 6
- drag: float32 [32768], P(('sector', 'axial')), may hold values from 0.5 to 5
- block_weight: float32 [32768], P(('sector', 'axial')), may hold values from 0.2 to 1
- flux_jac: float32 [3, 5, 5], replicated, may hold values from -2.5 to 2.5
- face_own: float32 [6, 5, 5], replicated, may hold values from -4 to 4
- face_nbr: float32 [6, 5, 5], replicated, may hold values from -4 to 4
- nbr_local: int32 [6, 32768], P(None, ('sector', 'axial')), may hold values from 0 to 1024, as said below
- sector_slots: int32 [2, 8192], P(None, ('sector', 'axial')), may hold values from 0 to 1023, as said below
- axial_slots: int32 [2, 8192], P(None, ('sector', 'axial')), may hold values from 0 to 1023, as said below
- sector_live: int32 [4, 8, 2], P('sector', 'axial'), may hold values from 128 to 256, as said below
- elem_block: int32 [32768], P(('sector', 'axial')), may hold values from 0 to 4095, as said below
Outputs:
- adjoint_next: float32 [5, 64, 32768], P(None, None, ('sector', 'axial'))
- block_grad: float32 [4096], P(('sector', 'axial'))
The draws below stay inside these ranges and needn't reach their ends.
Inputs may be any that keep to these rules, and one draw needn't show every extreme that they name: The elements of one device fill a block of 4 x 64 x 4 cells in some order; nbr_local is symmetric: across face f of element e lies face f xor 1 of element nbr_local[f, e]; the value 1024 marks faces on the device boundary. `sector_slots`: each row lists 256 distinct local elements of the device; slot s of one device's upper row and slot s of the next device's lower row are the two sides of one face with matching node order. `axial_slots`: each row lists 256 distinct local elements of the device; slot s of one device's upper row and slot s of the next slab's lower row are the two sides of one face with matching node order. `sector_live`: A device's upper count equals the lower count of the device one higher in sector index (cyclically). `elem_block`: the owner of an element's block (block // 128, in joint device order) is the element's own device or the one just before or after it, cyclically.
All inputs are finite; a program needn't handle non-finite values.
Results may differ from the reference program's by a relative error of at most 0.0006.
Values sent between devices are 32-bit elements; how exact they have to be, the bound alone decides.
A program may use at most 128 MiB of HBM per device.

```python
import math
import jax
import jax.numpy as jnp
import numpy as np
from jax import lax

FIELDS = 5
NODES = 64
SPAN = 4
RADIAL = 64
E_DEV = 1024
FACES = 256
SECTORS = 4
SLABS = 8
ELEMENTS = 32768
BLOCKS = 4096
BLK_DEV = 128


def cell_layout(key):
    devices = SECTORS * SLABS

    def one_device(device_id):
        return jax.random.permutation(jax.random.fold_in(jax.random.fold_in(key, 101), device_id), E_DEV).astype(jnp.int32)
    return jax.vmap(one_device)(jnp.arange(devices, dtype=jnp.int32))


def draw_nbr_local(key, part):
    devices = SECTORS * SLABS
    layout = cell_layout(key)
    cell_ids = jnp.arange(E_DEV, dtype=jnp.int32)
    along_x = cell_ids // (RADIAL * SPAN)
    along_y = cell_ids // SPAN % RADIAL
    along_z = cell_ids % SPAN
    neighbour_steps = [(along_x > 0, -RADIAL * SPAN), (along_x < SPAN - 1, RADIAL * SPAN), (along_y > 0, -SPAN), (along_y < RADIAL - 1, SPAN), (along_z > 0, -1), (along_z < SPAN - 1, 1)]
    device_rows = jnp.arange(devices, dtype=jnp.int32)[:, None]
    stacked_rows = []
    for present, offset in neighbour_steps:
        target = jnp.where(present, cell_ids + offset, 0)
        neighbour = jnp.where(present[None, :], layout[:, target], E_DEV)
        by_element = jnp.zeros_like(layout).at[device_rows, layout].set(neighbour)
        stacked_rows.append(by_element.reshape(-1))
    return jnp.stack(stacked_rows).astype(jnp.int32)


def draw_sector_slots(key, part):
    layout = cell_layout(key)
    slot_ids = jnp.arange(FACES, dtype=jnp.int32)
    lower_row = layout[:, slot_ids].reshape(-1)
    upper_row = layout[:, (SPAN - 1) * RADIAL * SPAN + slot_ids].reshape(-1)
    return jnp.stack([lower_row, upper_row]).astype(jnp.int32)


def draw_axial_slots(key, part):
    layout = cell_layout(key)
    slot_ids = jnp.arange(FACES, dtype=jnp.int32)
    lower_row = layout[:, slot_ids * SPAN].reshape(-1)
    upper_row = layout[:, slot_ids * SPAN + SPAN - 1].reshape(-1)
    return jnp.stack([lower_row, upper_row]).astype(jnp.int32)


def draw_sector_live(key, part):
    counts = jax.random.randint(jax.random.fold_in(key, 202), (SECTORS, SLABS), FACES // 2, FACES + 1).astype(jnp.int32)
    counts = counts.at[0].set(FACES).at[1].set(FACES // 2)
    return jnp.stack([jnp.roll(counts, 1, axis=0), counts], axis=-1).astype(jnp.int32)


def draw_elem_block(key, part):
    element_ids = jnp.arange(ELEMENTS, dtype=jnp.int32)
    device_ids = element_ids // E_DEV
    local_ids = element_ids % E_DEV
    offsets = jax.random.randint(jax.random.fold_in(key, 303), (ELEMENTS,), -BLK_DEV, 2 * BLK_DEV).astype(jnp.int32)
    offsets = jnp.where(local_ids == 0, -1, jnp.where(local_ids == 1, 0, offsets))
    return ((device_ids * BLK_DEV + offsets) % BLOCKS).astype(jnp.int32)


def block_scale(key, shape, cuts, least, high):
    loudness, own = 1.0, jax.random.fold_in(key, 6)
    for dim, parts in cuts:
        heights = jnp.exp(jax.random.uniform(jax.random.fold_in(own, dim), (parts,), jnp.float32, least / len(cuts), high / len(cuts)))
        loudness = loudness * jnp.repeat(heights, shape[dim] // parts).reshape([-1 if axis == dim else 1 for axis in range(len(shape))])
    return loudness


def scatter_about(stream_key, extent, spread, bound, pieces=(), kind=jnp.bfloat16):
    values = jax.random.normal(stream_key, extent, jnp.float32) * spread
    if len(pieces) > 0:
        values = block_scale(stream_key, extent, pieces, -0.22, 0.18) * values
    return jnp.clip(values, min=-bound, max=bound).astype(kind)


def setup_inputs(seed: int = 0) -> dict:
    splits = jax.random.split(jax.random.key(seed), 13)
    adjoint = scatter_about(splits[0], (FIELDS, NODES, ELEMENTS), 1.0, 6.0, ((2, 32),), jnp.float32)
    velocity = scatter_about(splits[1], (3, NODES, ELEMENTS), 1.0, 6.0, ((2, 32),))
    drag = jnp.clip(jnp.exp(math.log(5.0) - 2.3025851 * jax.random.uniform(splits[2], (ELEMENTS,), jnp.float32) ** block_scale(splits[2], (ELEMENTS,), ((0, 32),), -0.2, 0.2)), 0.5, 5.0)
    block_weight = jnp.clip(0.2 + 0.8 * jax.random.uniform(splits[3], (ELEMENTS,), jnp.float32) ** block_scale(splits[3], (ELEMENTS,), ((0, 32),), -0.2, 0.2), 0.2, 1.0)
    flux_jac = scatter_about(splits[4], (3, FIELDS, FIELDS), FIELDS ** -0.5, 2.5, (), jnp.float32)
    face_own = scatter_about(splits[5], (6, FIELDS, FIELDS), 1.0, 4.0, (), jnp.float32)
    face_nbr = scatter_about(splits[6], (6, FIELDS, FIELDS), 1.0, 4.0, (), jnp.float32)
    nbr_local = draw_nbr_local(jax.random.fold_in(splits[12], 71), 0)
    sector_slots = draw_sector_slots(jax.random.fold_in(splits[12], 71), 0)
    axial_slots = draw_axial_slots(jax.random.fold_in(splits[12], 71), 0)
    sector_live = draw_sector_live(jax.random.fold_in(splits[12], 71), 0)
    elem_block = draw_elem_block(jax.random.fold_in(splits[12], 71), 0)
    return dict(adjoint=adjoint, velocity=velocity, drag=drag, block_weight=block_weight, flux_jac=flux_jac, face_own=face_own, face_nbr=face_nbr, nbr_local=nbr_local, sector_slots=sector_slots, axial_slots=axial_slots, sector_live=sector_live, elem_block=elem_block)


PRECISE = lax.Precision.HIGHEST

def lobatto_tables():
    points = np.array([-1.0, -1.0 / np.sqrt(5.0), 1.0 / np.sqrt(5.0), 1.0])
    weights = np.array([1.0, 5.0, 5.0, 1.0]) / 6.0
    scales = np.array([np.prod([points[i] - points[k] for k in range(4) if k != i]) for i in range(4)])
    derivative = np.zeros((4, 4))
    for i in range(4):
        for p in range(4):
            if i != p:
                derivative[i, p] = scales[i] / scales[p] / (points[i] - points[p])
            else:
                derivative[i, p] = sum((1.0 / (points[i] - points[k]) for k in range(4) if k != i))
    node_weight = (weights[:, None, None] * weights[None, :, None] * weights[None, None, :]).reshape(64) / 8.0
    return (derivative, node_weight)

def volume_term(adjoint, flux_jac, derivative):
    fields, node_count, elem_count = adjoint.shape
    node_cube = adjoint.reshape(fields, 4, 4, 4, elem_count)
    along_a = jnp.einsum('pi,hpbge->hibge', derivative, node_cube, precision=PRECISE)
    along_b = jnp.einsum('pi,hapge->haige', derivative, node_cube, precision=PRECISE)
    along_g = jnp.einsum('pi,habpe->habie', derivative, node_cube, precision=PRECISE)
    stacked = jnp.stack([along_a, along_b, along_g]).reshape(3, fields, node_count, elem_count)
    return jnp.einsum('dhc,dhne->cne', flux_jac, stacked, precision=PRECISE)

def face_traces(adjoint):
    fields, node_count, elem_count = adjoint.shape
    node_cube = adjoint.reshape(fields, 4, 4, 4, elem_count)
    face_slabs = [node_cube[:, 0], node_cube[:, 3], node_cube[:, :, 0], node_cube[:, :, 3], node_cube[:, :, :, 0], node_cube[:, :, :, 3]]
    return jnp.stack([slab.reshape(fields, 16, elem_count) for slab in face_slabs])

def lift_faces(surface):
    face_count, fields, face_nodes, elem_count = surface.shape
    face_tiles = surface.reshape(6, fields, 4, 4, elem_count)
    node_cube = jnp.zeros((fields, 4, 4, 4, elem_count), jnp.float32)
    node_cube = node_cube.at[:, 0].add(face_tiles[0]).at[:, 3].add(face_tiles[1])
    node_cube = node_cube.at[:, :, 0].add(face_tiles[2]).at[:, :, 3].add(face_tiles[3])
    node_cube = node_cube.at[:, :, :, 0].add(face_tiles[4]).at[:, :, :, 3].add(face_tiles[5])
    return node_cube.reshape(fields, 64, elem_count)

def finish_update(adjoint, velocity, drag, nbr_local, sector_slots, axial_slots, live_counts, received, flux_jac, face_own, face_nbr):
    derivative_np, weight_np = lobatto_tables()
    derivative = jnp.asarray(derivative_np, dtype=jnp.float32)
    node_weight = jnp.asarray(weight_np, dtype=jnp.float32)
    fields, node_count, elem_count = adjoint.shape
    traces = face_traces(adjoint)
    inside = nbr_local < elem_count
    clamped = jnp.where(inside, nbr_local, 0)
    partners = []
    for face_id in range(6):
        partner_tr = jnp.take(traces[face_id ^ 1], clamped[face_id], axis=2)
        partners.append(jnp.where(inside[face_id][None, None, :], partner_tr, 0.0))
    slot_count = sector_slots.shape[1]
    positions = jnp.arange(slot_count, dtype=jnp.int32)
    mask_low = (positions < live_counts[0]).astype(jnp.float32)
    mask_high = (positions < live_counts[1]).astype(jnp.float32)
    from_x_below, from_x_above, from_z_below, from_z_above = received

    def place(partner_face, arrived, slot_list, weight_mask):
        values = (arrived * weight_mask[None, :]).reshape(fields, 16, slot_count)
        return partner_face.at[:, :, slot_list].add(values)
    partners[0] = place(partners[0], from_x_below, sector_slots[0], mask_low)
    partners[1] = place(partners[1], from_x_above, sector_slots[1], mask_high)
    ones_mask = jnp.ones((slot_count,), jnp.float32)
    partners[4] = place(partners[4], from_z_below, axial_slots[0], ones_mask)
    partners[5] = place(partners[5], from_z_above, axial_slots[1], ones_mask)
    partner_all = jnp.stack(partners)
    surface = jnp.einsum('fch,fhme->fcme', face_own, traces, precision=PRECISE) + jnp.einsum('fch,fhme->fcme', face_nbr, partner_all, precision=PRECISE)
    field_mask = jnp.array([0.0, 1.0, 1.0, 1.0, 0.0], dtype=jnp.float32)
    damping = field_mask[:, None, None] * drag[None, None, :]
    tendency = volume_term(adjoint, flux_jac, derivative) + lift_faces(surface) - damping * adjoint
    adjoint_next = adjoint + 0.1 * tendency
    velocity_f = velocity.astype(jnp.float32)
    elem_grad = drag * lax.optimization_barrier(jnp.sum(adjoint[1:4] * velocity_f * node_weight[None, :, None], axis=(0, 1)))
    return (adjoint_next, elem_grad)

def reference(adjoint, velocity, drag, block_weight, flux_jac, face_own, face_nbr, nbr_local, sector_slots, axial_slots, sector_live, elem_block):
    fields = adjoint.shape[0]
    devices = SECTORS * SLABS
    node_cube = adjoint.reshape(fields, 4, 4, 4, ELEMENTS)
    base_index = (jnp.arange(devices, dtype=jnp.int32) * E_DEV)[:, None]

    def edge(tile, slot_row):
        gathered = (base_index + slot_row.reshape(devices, FACES).astype(jnp.int32)).reshape(-1)
        picked = jnp.take(tile.reshape(fields * 16, ELEMENTS), gathered, axis=1)
        return picked.reshape(fields * 16, SECTORS, SLABS, FACES)
    low_x = edge(node_cube[:, 0], sector_slots[0])
    high_x = edge(node_cube[:, 3], sector_slots[1])
    low_z = edge(node_cube[:, :, :, 0], axial_slots[0])
    high_z = edge(node_cube[:, :, :, 3], axial_slots[1])
    from_x_below = jnp.roll(high_x, 1, axis=1)
    from_x_above = jnp.roll(low_x, -1, axis=1)
    zero_slab = jnp.zeros_like(high_z[:, :, :1])
    from_z_below = jnp.concatenate([zero_slab, high_z[:, :, :-1]], axis=2)
    from_z_above = jnp.concatenate([low_z[:, :, 1:], zero_slab], axis=2)
    recv_all = [stacked_arr.reshape(fields * 16, devices, FACES) for stacked_arr in (from_x_below, from_x_above, from_z_below, from_z_above)]
    live_all = sector_live.reshape(devices, 2)
    nbr_all = nbr_local.reshape(6, devices, E_DEV)
    sector_all = sector_slots.reshape(2, devices, FACES)
    axial_all = axial_slots.reshape(2, devices, FACES)

    def visit_device(device_q, carry):
        result, elem_grads = carry
        first_col = device_q * E_DEV

        def select_device(stacked_arr):
            return lax.dynamic_index_in_dim(stacked_arr, device_q, 1, False)
        own_state = lax.dynamic_slice_in_dim(adjoint, first_col, E_DEV, 2)
        own_velocity = lax.dynamic_slice_in_dim(velocity, first_col, E_DEV, 2)
        own_drag = lax.dynamic_slice_in_dim(drag, first_col, E_DEV, 0)
        received = tuple((select_device(stacked_arr) for stacked_arr in recv_all))
        live_counts = lax.dynamic_index_in_dim(live_all, device_q, 0, False)
        state_next, grad_part = finish_update(own_state, own_velocity, own_drag, select_device(nbr_all), select_device(sector_all), select_device(axial_all), live_counts, received, flux_jac, face_own, face_nbr)
        result = lax.dynamic_update_slice_in_dim(result, state_next, first_col, 2)
        elem_grads = lax.dynamic_update_slice_in_dim(elem_grads, grad_part, first_col, 0)
        return (result, elem_grads)
    adjoint_next, elem_grads = lax.fori_loop(0, devices, visit_device, (jnp.zeros_like(adjoint), jnp.zeros((ELEMENTS,), jnp.float32)))
    block_grad = jax.ops.segment_sum(block_weight * elem_grads, elem_block, num_segments=BLOCKS)
    return (adjoint_next, block_grad)
```

```python
import functools

import jax
import jax.numpy as jnp
import numpy as np
from jax import lax
from jax.experimental import pallas as pl
from jax.experimental.pallas import tpu as pltpu
from jax.sharding import PartitionSpec as P

BLOCKS = 4096
BF = jnp.bfloat16
F32 = jnp.float32
MESH = pl.DeviceIdType.MESH


def lobatto_tables():
    points = np.array([-1.0, -1.0 / np.sqrt(5.0), 1.0 / np.sqrt(5.0), 1.0])
    weights = np.array([1.0, 5.0, 5.0, 1.0]) / 6.0
    scales = np.array(
        [np.prod([points[i] - points[k] for k in range(4) if k != i]) for i in range(4)]
    )
    derivative = np.zeros((4, 4))
    for i in range(4):
        for p in range(4):
            if i != p:
                derivative[i, p] = scales[i] / scales[p] / (points[i] - points[p])
            else:
                derivative[i, p] = sum((1.0 / (points[i] - points[k]) for k in range(4) if k != i))
    node_weight = (
        weights[:, None, None] * weights[None, :, None] * weights[None, None, :]
    ).reshape(64) / 8.0
    return (derivative, node_weight)


def constant_tables():
    derivative, node_weight = lobatto_tables()
    eye = np.eye(4)
    step = derivative.T
    along = [
        np.kron(np.kron(step, eye), eye),
        np.kron(np.kron(eye, step), eye),
        np.kron(np.kron(eye, eye), step),
    ]
    nodes = np.arange(64).reshape(4, 4, 4)
    faces = [nodes[0], nodes[3], nodes[:, 0], nodes[:, 3], nodes[:, :, 0], nodes[:, :, 3]]
    faces = [f.reshape(16) for f in faces]
    mats = list(along)
    pick = np.zeros((96, 64))
    lift = np.zeros((64, 512))
    for f, ids in enumerate(faces):
        diag = np.zeros((64, 64))
        diag[ids, ids] = 1.0
        mats.append(diag)
        pick[16 * f + np.arange(16), ids] = 1.0
        for h in range(5):
            lift[ids, 80 * f + 16 * h + np.arange(16)] = 0.1
    mats = 0.1 * np.stack([np.concatenate([m, m], axis=1) for m in mats])
    spread = np.zeros((8, 384))
    for h in range(5):
        spread[h, 64 * h : 64 * h + 64] = 1.0
    spread_nbr = np.zeros((32, 512))
    for k in range(30):
        spread_nbr[k, 16 * k : 16 * k + 16] = 1.0
    weight = np.repeat(node_weight[:, None], 128, axis=1)
    return (
        jnp.asarray(mats, F32),
        jnp.asarray(pick, BF),
        jnp.asarray(lift, F32),
        jnp.asarray(spread, F32),
        jnp.asarray(spread_nbr, F32),
        jnp.asarray(weight, F32),
    )


def split2(x):
    hi = x.astype(BF)
    return hi, (x - hi.astype(F32)).astype(BF)


def dot(a, b):
    return jnp.dot(a, b, preferred_element_type=F32)


def dot_nt(a, b):
    return lax.dot_general(a, b, (((1,), (1,)), ((), ())), preferred_element_type=F32)


def one_hot(mask):
    return jnp.where(mask, 1.0, 0.0).astype(BF)


def kernel(
    sectors,
    slabs,
    owned,
    x_ref,
    vel_ref,
    drag_ref,
    bw_ref,
    coef_ref,
    nbr_ref,
    sslots_ref,
    aslots_ref,
    live_ref,
    eb_ref,
    mats_ref,
    pick_ref,
    lift_ref,
    spread_ref,
    spread_nbr_ref,
    weight_ref,
    out_ref,
    grad_ref,
    xs_ref,
    tr_ref,
    oh_ref,
    send_ref,
    recv_ref,
    part_ref,
    ps_ref,
    a_ref,
    b_ref,
    bsend_ref,
    brecv_ref,
    send_sem,
    recv_sem,
):
    elems = x_ref.shape[2]
    slots = sslots_ref.shape[1]
    width = bsend_ref.shape[2]
    count = sectors * slabs
    sec = lax.axis_index("sector")
    axi = lax.axis_index("axial")
    joint = sec * slabs + axi
    prev = lax.rem(joint + count - 1, count)
    nxt = lax.rem(joint + 1, count)
    dev_prev = (prev // slabs, lax.rem(prev, slabs))
    dev_next = (nxt // slabs, lax.rem(nxt, slabs))
    dev_low = (lax.rem(sec + sectors - 1, sectors), axi)
    dev_high = (lax.rem(sec + 1, sectors), axi)

    barrier = pltpu.get_barrier_semaphore()
    for device in (dev_prev, dev_next, dev_low, dev_high):
        pl.semaphore_signal(barrier, inc=1, device_id=device, device_id_type=MESH)

    for h in range(5):
        hi, lo = split2(x_ref[h])
        xs_ref[0, 64 * h : 64 * h + 64, :] = hi
        xs_ref[1, 64 * h : 64 * h + 64, :] = lo
        for s, half in enumerate((hi, lo)):
            picked = dot(pick_ref[...], half).astype(BF)
            for f in range(6):
                row = 80 * s + 16 * h
                tr_ref[f, row : row + 16, :] = picked[16 * f : 16 * f + 16, :]
    xs_ref[0, 320:384, :] = jnp.zeros((64, elems), BF)
    xs_ref[1, 320:384, :] = jnp.zeros((64, elems), BF)

    rows_slots = lax.broadcasted_iota(jnp.int32, (elems, slots), 0)
    sides = ((0, sslots_ref, 0), (1, sslots_ref, 1), (4, aslots_ref, 0), (5, aslots_ref, 1))
    for i, (face, ref, row) in enumerate(sides):
        hot = one_hot(rows_slots == ref[row : row + 1, :])
        oh_ref[i] = hot
        both = dot(tr_ref[face], hot)
        send_ref[i] = both[:80] + both[80:]

    pl.semaphore_wait(barrier, 4)

    def remote(src, dst, k, device):
        return pltpu.make_async_remote_copy(
            src_ref=src,
            dst_ref=dst,
            send_sem=send_sem.at[k],
            recv_sem=recv_sem.at[k],
            device_id=device,
            device_id_type=MESH,
        )

    up_x = remote(send_ref.at[1], recv_ref.at[0], 0, dev_high)
    down_x = remote(send_ref.at[0], recv_ref.at[1], 1, dev_low)
    up_z = remote(send_ref.at[3], recv_ref.at[2], 2, dev_next)
    down_z = remote(send_ref.at[2], recv_ref.at[3], 3, dev_prev)
    up_b = remote(bsend_ref.at[2], brecv_ref.at[0], 4, dev_next)
    down_b = remote(bsend_ref.at[0], brecv_ref.at[1], 5, dev_prev)
    has_low = axi > 0
    has_high = axi < slabs - 1
    up_x.start()
    down_x.start()

    @pl.when(has_high)
    def _():
        up_z.start()

    @pl.when(has_low)
    def _():
        down_z.start()

    @pl.when(jnp.logical_not(has_low))
    def _():
        recv_ref[2] = jnp.zeros((80, slots), F32)

    @pl.when(jnp.logical_not(has_high))
    def _():
        recv_ref[3] = jnp.zeros((80, slots), F32)

    drag = drag_ref[...]
    acc = x_ref[1] * vel_ref[0].astype(F32)
    acc += x_ref[2] * vel_ref[1].astype(F32)
    acc += x_ref[3] * vel_ref[2].astype(F32)
    elem_grad = drag * jnp.sum(acc * weight_ref[:, 0:1], axis=0, keepdims=True)
    weighted = bw_ref[...] * elem_grad
    w1 = weighted.astype(BF)
    rest = weighted - w1.astype(F32)
    w2 = rest.astype(BF)
    w3 = (rest - w2.astype(F32)).astype(BF).astype(F32)
    row16 = lax.broadcasted_iota(jnp.int32, (16, elems), 0)
    stack = jnp.where(row16 == 0, w1.astype(F32), 0.0)
    stack = jnp.where(row16 == 1, w2.astype(F32), stack)
    stack = jnp.where(row16 == 2, w3, stack).astype(BF)
    rel = eb_ref[...] - (joint - 1) * owned
    rel = jnp.where(rel < 0, rel + BLOCKS, rel)
    rel = jnp.where(rel >= BLOCKS, rel - BLOCKS, rel)
    rows_blk = lax.broadcasted_iota(jnp.int32, (width, elems), 0)
    for j in range(3):
        sums = dot_nt(stack, one_hot(rows_blk == rel - j * owned))
        total = jnp.sum(sums, axis=0, keepdims=True)
        bsend_ref[j] = jnp.broadcast_to(total, (8, width))
    up_b.start()
    down_b.start()

    rowc = []
    for j in range(9):
        cols = coef_ref[j]
        row = cols[:, 0:1] * spread_ref[0:1, :]
        for h in range(1, 5):
            row += cols[:, h : h + 1] * spread_ref[h : h + 1, :]
        rowc.append(row)
    rown = jnp.zeros((5, 512), F32)
    for f in range(6):
        cols = coef_ref[9 + f]
        for h in range(5):
            k = 5 * f + h
            rown += cols[:, h : h + 1] * spread_nbr_ref[k : k + 1, :]
    for c in range(5):
        rows = slice(64 * c, 64 * c + 64)
        for t in range(3):
            lanes = slice(128 * t, 128 * t + 128)
            total = mats_ref[0] * rowc[0][c : c + 1, lanes]
            for j in range(1, 9):
                total += mats_ref[j] * rowc[j][c : c + 1, lanes]
            a_ref[0, rows, lanes], a_ref[1, rows, lanes] = split2(total)
        b_ref[0, rows, :], b_ref[1, rows, :] = split2(lift_ref[...] * rown[c : c + 1, :])

    own = dot(a_ref[0], xs_ref[0]) + dot(a_ref[0], xs_ref[1]) + dot(a_ref[1], xs_ref[0])
    keep = 1.0 - 0.1 * drag
    for c in range(5):
        x = x_ref[c]
        scaled = x * keep if 1 <= c <= 3 else x
        out_ref[c] = scaled + own[64 * c : 64 * c + 64, :]

    chunk = 256
    rows_src = lax.broadcasted_iota(jnp.int32, (chunk, elems), 0)

    def gather(f, carry):
        ids = nbr_ref[pl.ds(f, 1), :]
        g = f + 1 - 2 * lax.rem(f, 2)
        both = jnp.zeros((160, elems), F32)
        for k in range(elems // chunk):
            hot = one_hot(rows_src == ids - k * chunk)
            both += dot(tr_ref[g, :, k * chunk : (k + 1) * chunk], hot)
        part_ref[f] = both[:80] + both[80:]
        return carry

    lax.fori_loop(0, 6, gather, 0)

    up_x.wait()
    down_x.wait()

    @pl.when(has_high)
    def _():
        up_z.wait_send()
        down_z.wait_recv()

    @pl.when(has_low)
    def _():
        down_z.wait_send()
        up_z.wait_recv()

    slot_ids = lax.broadcasted_iota(jnp.int32, (80, slots), 1)
    for i, face in enumerate((0, 1, 4, 5)):
        got = recv_ref[i]
        if i < 2:
            got = jnp.where(slot_ids < live_ref[0, i], got, 0.0)
        both = dot_nt(jnp.concatenate(split2(got), axis=0), oh_ref[i])
        part_ref[face] += both[:80] + both[80:]
    for f in range(6):
        rows = slice(80 * f, 80 * f + 80)
        ps_ref[0, rows, :], ps_ref[1, rows, :] = split2(part_ref[f])
    for s in range(2):
        ps_ref[s, 480:512, :] = jnp.zeros((32, elems), BF)
    nbr = dot(b_ref[0], ps_ref[0]) + dot(b_ref[0], ps_ref[1]) + dot(b_ref[1], ps_ref[0])
    for c in range(5):
        out_ref[c] += nbr[64 * c : 64 * c + 64, :]

    up_b.wait()
    down_b.wait()
    sums = bsend_ref[1] + brecv_ref[0] + brecv_ref[1]
    grad_ref[...] = sums[0:1, :owned]


def on_device(
    sectors,
    slabs,
    adjoint,
    velocity,
    drag,
    block_weight,
    flux_jac,
    face_own,
    face_nbr,
    nbr_local,
    sector_slots,
    axial_slots,
    sector_live,
    elem_block,
):
    elems = adjoint.shape[2]
    slots = sector_slots.shape[1]
    owned = BLOCKS // (sectors * slabs)
    width = -(-owned // 128) * 128
    coef = jnp.concatenate([jnp.swapaxes(flux_jac, 1, 2), face_own, face_nbr])
    vmem = pl.BlockSpec(memory_space=pltpu.VMEM)
    smem = pl.BlockSpec(memory_space=pltpu.SMEM)
    out, grad = pl.pallas_call(
        functools.partial(kernel, sectors, slabs, owned),
        out_shape=(
            jax.ShapeDtypeStruct(adjoint.shape, F32),
            jax.ShapeDtypeStruct((1, owned), F32),
        ),
        in_specs=[vmem] * 8 + [smem] + [vmem] * 7,
        out_specs=(vmem, vmem),
        scratch_shapes=[
            pltpu.VMEM((2, 384, elems), BF),
            pltpu.VMEM((6, 160, elems), BF),
            pltpu.VMEM((4, elems, slots), BF),
            pltpu.VMEM((4, 80, slots), F32),
            pltpu.VMEM((4, 80, slots), F32),
            pltpu.VMEM((6, 80, elems), F32),
            pltpu.VMEM((2, 512, elems), BF),
            pltpu.VMEM((2, 320, 384), BF),
            pltpu.VMEM((2, 320, 512), BF),
            pltpu.VMEM((3, 8, width), F32),
            pltpu.VMEM((2, 8, width), F32),
            pltpu.SemaphoreType.DMA((6,)),
            pltpu.SemaphoreType.DMA((6,)),
        ],
        compiler_params=pltpu.CompilerParams(
            collective_id=0, has_side_effects=True, vmem_limit_bytes=48 * 1024 * 1024
        ),
    )(
        adjoint,
        velocity,
        drag.reshape(1, elems),
        block_weight.reshape(1, elems),
        coef,
        nbr_local,
        sector_slots,
        axial_slots,
        sector_live.reshape(1, 2),
        elem_block.reshape(1, elems),
        *constant_tables(),
    )
    return out, grad.reshape(owned)


def solution(mesh):
    placed = (
        P(None, None, ("sector", "axial")),
        P(None, None, ("sector", "axial")),
        P(("sector", "axial")),
        P(("sector", "axial")),
        P(),
        P(),
        P(),
        P(None, ("sector", "axial")),
        P(None, ("sector", "axial")),
        P(None, ("sector", "axial")),
        P("sector", "axial", None),
        P(("sector", "axial")),
    )
    return jax.shard_map(
        functools.partial(on_device, mesh.shape["sector"], mesh.shape["axial"]),
        mesh=mesh,
        in_specs=placed,
        out_specs=(P(None, None, ("sector", "axial")), P(("sector", "axial"))),
        check_vma=False,
    )
```

```python
import functools

import jax
import jax.numpy as jnp
import numpy as np
from jax import lax
from jax.experimental import pallas as pl
from jax.experimental.pallas import tpu as pltpu
from jax.sharding import PartitionSpec as P

BLOCKS = 4096
BF = jnp.bfloat16
F32 = jnp.float32
MESH = pl.DeviceIdType.MESH
INPUTS = 15


def lobatto_tables():
    points = np.array([-1.0, -1.0 / np.sqrt(5.0), 1.0 / np.sqrt(5.0), 1.0])
    weights = np.array([1.0, 5.0, 5.0, 1.0]) / 6.0
    scales = np.array(
        [np.prod([points[i] - points[k] for k in range(4) if k != i]) for i in range(4)]
    )
    derivative = np.zeros((4, 4))
    for i in range(4):
        for p in range(4):
            if i != p:
                derivative[i, p] = scales[i] / scales[p] / (points[i] - points[p])
            else:
                derivative[i, p] = sum((1.0 / (points[i] - points[k]) for k in range(4) if k != i))
    node_weight = (
        weights[:, None, None] * weights[None, :, None] * weights[None, None, :]
    ).reshape(64) / 8.0
    return (derivative, node_weight)


def constant_tables():
    derivative, node_weight = lobatto_tables()
    eye = np.eye(4)
    step = derivative.T
    along = [
        np.kron(np.kron(step, eye), eye),
        np.kron(np.kron(eye, step), eye),
        np.kron(np.kron(eye, eye), step),
    ]
    nodes = np.arange(64).reshape(4, 4, 4)
    faces = [nodes[0], nodes[3], nodes[:, 0], nodes[:, 3], nodes[:, :, 0], nodes[:, :, 3]]
    faces = [f.reshape(16) for f in faces]
    mats = list(along)
    pick = np.zeros((96, 64))
    lift = np.zeros((64, 512))
    for f, ids in enumerate(faces):
        diag = np.zeros((64, 64))
        diag[ids, ids] = 1.0
        mats.append(diag)
        pick[16 * f + np.arange(16), ids] = 1.0
        for h in range(5):
            lift[ids, 80 * f + 16 * h + np.arange(16)] = 0.1
    mats = [0.1 * np.concatenate([m, m], axis=1) for m in mats]
    mats.append(np.repeat(node_weight[:, None], 128, axis=1))
    return (
        jnp.asarray(np.stack(mats), F32),
        jnp.asarray(pick, BF),
        jnp.asarray(lift, F32),
    )


def split2(x):
    hi = x.astype(BF)
    return hi, (x - hi.astype(F32)).astype(BF)


def dot(a, b):
    return jnp.dot(a, b, preferred_element_type=F32)


def dot_nt(a, b):
    return lax.dot_general(a, b, (((1,), (1,)), ((), ())), preferred_element_type=F32)


def one_hot(mask):
    return jnp.where(mask, 1.0, 0.0).astype(BF)


def kernel(
    sectors,
    slabs,
    owned,
    *refs,
):
    hbm_refs = refs[:INPUTS]
    out_ref, grad_ref = refs[INPUTS : INPUTS + 2]
    vmem_refs = refs[INPUTS + 2 : 2 * INPUTS + 2]
    rest_refs = refs[2 * INPUTS + 2 :]
    (
        x_ref,
        vel_ref,
        drag_ref,
        bw_ref,
        jac_ref,
        own_ref,
        nbrmat_ref,
        nbr_ref,
        sslots_ref,
        aslots_ref,
        live_ref,
        eb_ref,
        mats_ref,
        pick_ref,
        lift_ref,
    ) = vmem_refs
    (
        xs_ref,
        tr_ref,
        oh_ref,
        send_ref,
        recv_ref,
        part_ref,
        ps_ref,
        a_ref,
        b_ref,
        bsend_ref,
        brecv_ref,
        send_sem,
        recv_sem,
        load_sem,
    ) = rest_refs
    loads = {
        k: pltpu.make_async_copy(hbm_refs[k], vmem_refs[k], load_sem.at[k])
        for k in range(1, INPUTS)
    }
    fields = [
        pltpu.make_async_copy(hbm_refs[0].at[h], x_ref.at[h], load_sem.at[INPUTS + h])
        for h in range(5)
    ]
    for k in (13, 8, 9):
        loads[k].start()
    for field in fields:
        field.start()
    for k in (1, 2, 3, 11, 12, 4, 5, 6, 14, 7, 10):
        loads[k].start()
    elems = x_ref.shape[2]
    slots = sslots_ref.shape[1]
    width = bsend_ref.shape[2]
    count = sectors * slabs
    sec = lax.axis_index("sector")
    axi = lax.axis_index("axial")
    joint = sec * slabs + axi
    prev = lax.rem(joint + count - 1, count)
    nxt = lax.rem(joint + 1, count)
    dev_prev = (prev // slabs, lax.rem(prev, slabs))
    dev_next = (nxt // slabs, lax.rem(nxt, slabs))
    dev_low = (lax.rem(sec + sectors - 1, sectors), axi)
    dev_high = (lax.rem(sec + 1, sectors), axi)

    barrier = pltpu.get_barrier_semaphore()
    for device in (dev_prev, dev_next, dev_low, dev_high):
        pl.semaphore_signal(barrier, inc=1, device_id=device, device_id_type=MESH)

    loads[13].wait()
    for h in range(5):
        fields[h].wait()
        hi, lo = split2(x_ref[h])
        xs_ref[0, 64 * h : 64 * h + 64, :] = hi
        xs_ref[1, 64 * h : 64 * h + 64, :] = lo
        for s, half in enumerate((hi, lo)):
            picked = dot(pick_ref[...], half).astype(BF)
            for f in range(6):
                row = 80 * s + 16 * h
                tr_ref[f, row : row + 16, :] = picked[16 * f : 16 * f + 16, :]
    xs_ref[0, 320:384, :] = jnp.zeros((64, elems), BF)
    xs_ref[1, 320:384, :] = jnp.zeros((64, elems), BF)

    loads[8].wait()
    loads[9].wait()
    rows_slots = lax.broadcasted_iota(jnp.int32, (elems, slots), 0)
    sides = ((0, sslots_ref, 0), (1, sslots_ref, 1), (4, aslots_ref, 0), (5, aslots_ref, 1))
    for i, (face, ref, row) in enumerate(sides):
        hot = one_hot(rows_slots == ref[row : row + 1, :])
        oh_ref[i] = hot
        both = dot(tr_ref[face], hot)
        send_ref[i] = both[:80] + both[80:]

    pl.semaphore_wait(barrier, 4)

    def remote(src, dst, k, device):
        return pltpu.make_async_remote_copy(
            src_ref=src,
            dst_ref=dst,
            send_sem=send_sem.at[k],
            recv_sem=recv_sem.at[k],
            device_id=device,
            device_id_type=MESH,
        )

    up_x = remote(send_ref.at[1], recv_ref.at[0], 0, dev_high)
    down_x = remote(send_ref.at[0], recv_ref.at[1], 1, dev_low)
    up_z = remote(send_ref.at[3], recv_ref.at[2], 2, dev_next)
    down_z = remote(send_ref.at[2], recv_ref.at[3], 3, dev_prev)
    up_b = remote(bsend_ref.at[2], brecv_ref.at[0], 4, dev_next)
    down_b = remote(bsend_ref.at[0], brecv_ref.at[1], 5, dev_prev)
    has_low = axi > 0
    has_high = axi < slabs - 1
    up_x.start()
    down_x.start()

    @pl.when(has_high)
    def _():
        up_z.start()

    @pl.when(has_low)
    def _():
        down_z.start()

    @pl.when(jnp.logical_not(has_low))
    def _():
        recv_ref[2] = jnp.zeros((80, slots), F32)

    @pl.when(jnp.logical_not(has_high))
    def _():
        recv_ref[3] = jnp.zeros((80, slots), F32)

    for k in (1, 2, 3, 11, 12):
        loads[k].wait()
    drag = drag_ref[...]
    acc = x_ref[1] * vel_ref[0].astype(F32)
    acc += x_ref[2] * vel_ref[1].astype(F32)
    acc += x_ref[3] * vel_ref[2].astype(F32)
    elem_grad = drag * jnp.sum(acc * mats_ref[9][:, 0:1], axis=0, keepdims=True)
    weighted = bw_ref[...] * elem_grad
    w1 = weighted.astype(BF)
    rest = weighted - w1.astype(F32)
    w2 = rest.astype(BF)
    w3 = (rest - w2.astype(F32)).astype(BF).astype(F32)
    row16 = lax.broadcasted_iota(jnp.int32, (16, elems), 0)
    stack = jnp.where(row16 == 0, w1.astype(F32), 0.0)
    stack = jnp.where(row16 == 1, w2.astype(F32), stack)
    stack = jnp.where(row16 == 2, w3, stack).astype(BF)
    rel = eb_ref[...] - (joint - 1) * owned
    rel = jnp.where(rel < 0, rel + BLOCKS, rel)
    rel = jnp.where(rel >= BLOCKS, rel - BLOCKS, rel)
    rows_blk = lax.broadcasted_iota(jnp.int32, (width, elems), 0)
    for j in range(3):
        sums = dot_nt(stack, one_hot(rows_blk == rel - j * owned))
        total = jnp.sum(sums, axis=0, keepdims=True)
        bsend_ref[j] = jnp.broadcast_to(total, (8, width))
    up_b.start()
    down_b.start()

    for k in (4, 5, 6, 14):
        loads[k].wait()
    spread = lax.broadcasted_iota(jnp.int32, (5, 384), 1) // 64
    spread = jnp.where(spread == lax.broadcasted_iota(jnp.int32, (5, 384), 0), 1.0, 0.0)
    lane = lax.broadcasted_iota(jnp.int32, (6, 512), 1)
    face_row = lax.broadcasted_iota(jnp.int32, (6, 512), 0)
    slot_row = lane // 16 - 5 * face_row
    for c in range(5):
        rows = slice(64 * c, 64 * c + 64)
        jac = jac_ref[0][:, c : c + 1] * spread[0:1, :]
        face = own_ref[c][:, 0:1] * spread[0:1, :]
        nbrs = jnp.where(slot_row == 0, nbrmat_ref[c][:, 0:1], 0.0)
        for h in range(1, 5):
            jac += jac_ref[h][:, c : c + 1] * spread[h : h + 1, :]
            face += own_ref[c][:, h : h + 1] * spread[h : h + 1, :]
            nbrs = jnp.where(slot_row == h, nbrmat_ref[c][:, h : h + 1], nbrs)
        rown = jnp.sum(nbrs, axis=0, keepdims=True)
        for t in range(3):
            lanes = slice(128 * t, 128 * t + 128)
            total = mats_ref[0] * jac[0:1, lanes]
            for j in range(1, 9):
                row = jac[j : j + 1, lanes] if j < 3 else face[j - 3 : j - 2, lanes]
                total += mats_ref[j] * row
            a_ref[0, rows, lanes], a_ref[1, rows, lanes] = split2(total)
        b_ref[0, rows, :], b_ref[1, rows, :] = split2(lift_ref[...] * rown)

    own = dot(a_ref[0], xs_ref[0]) + dot(a_ref[0], xs_ref[1]) + dot(a_ref[1], xs_ref[0])
    keep = 1.0 - 0.1 * drag
    for c in range(5):
        x = x_ref[c]
        scaled = x * keep if 1 <= c <= 3 else x
        out_ref[c] = scaled + own[64 * c : 64 * c + 64, :]

    loads[7].wait()
    chunk = 256
    rows_src = lax.broadcasted_iota(jnp.int32, (chunk, elems), 0)

    def gather(f, carry):
        ids = nbr_ref[pl.ds(f, 1), :]
        g = f + 1 - 2 * lax.rem(f, 2)
        both = jnp.zeros((160, elems), F32)
        for k in range(elems // chunk):
            hot = one_hot(rows_src == ids - k * chunk)
            both += dot(tr_ref[g, :, k * chunk : (k + 1) * chunk], hot)
        part_ref[f] = both[:80] + both[80:]
        return carry

    lax.fori_loop(0, 6, gather, 0)

    up_x.wait()
    down_x.wait()

    @pl.when(has_high)
    def _():
        up_z.wait_send()
        down_z.wait_recv()

    @pl.when(has_low)
    def _():
        down_z.wait_send()
        up_z.wait_recv()

    loads[10].wait()
    slot_ids = lax.broadcasted_iota(jnp.int32, (80, slots), 1)
    for i, face in enumerate((0, 1, 4, 5)):
        got = recv_ref[i]
        if i < 2:
            got = jnp.where(slot_ids < live_ref[:, i : i + 1], got, 0.0)
        both = dot_nt(jnp.concatenate(split2(got), axis=0), oh_ref[i])
        part_ref[face] += both[:80] + both[80:]
    for f in range(6):
        rows = slice(80 * f, 80 * f + 80)
        ps_ref[0, rows, :], ps_ref[1, rows, :] = split2(part_ref[f])
    for s in range(2):
        ps_ref[s, 480:512, :] = jnp.zeros((32, elems), BF)
    nbr = dot(b_ref[0], ps_ref[0]) + dot(b_ref[0], ps_ref[1]) + dot(b_ref[1], ps_ref[0])
    for c in range(5):
        out_ref[c] += nbr[64 * c : 64 * c + 64, :]

    up_b.wait()
    down_b.wait()
    sums = bsend_ref[1] + brecv_ref[0] + brecv_ref[1]
    grad_ref[...] = sums[0, :owned]


def on_device(
    sectors,
    slabs,
    adjoint,
    velocity,
    drag,
    block_weight,
    flux_jac,
    face_own,
    face_nbr,
    nbr_local,
    sector_slots,
    axial_slots,
    sector_live,
    elem_block,
):
    elems = adjoint.shape[2]
    slots = sector_slots.shape[1]
    owned = BLOCKS // (sectors * slabs)
    width = -(-owned // 128) * 128
    operands = (
        adjoint,
        velocity,
        drag.reshape(1, elems),
        block_weight.reshape(1, elems),
        jnp.transpose(flux_jac, (1, 0, 2)),
        jnp.transpose(face_own, (1, 0, 2)),
        jnp.transpose(face_nbr, (1, 0, 2)),
        nbr_local,
        sector_slots,
        axial_slots,
        sector_live.reshape(1, 2),
        elem_block.reshape(1, elems),
        *constant_tables(),
    )
    vmem = pl.BlockSpec(memory_space=pltpu.VMEM)
    hbm = pl.BlockSpec(memory_space=pltpu.HBM)
    out, grad = pl.pallas_call(
        functools.partial(kernel, sectors, slabs, owned),
        out_shape=(
            jax.ShapeDtypeStruct(adjoint.shape, F32),
            jax.ShapeDtypeStruct((owned,), F32),
        ),
        in_specs=[hbm] * INPUTS,
        out_specs=(vmem, vmem),
        scratch_shapes=[pltpu.VMEM(a.shape, a.dtype) for a in operands]
        + [
            pltpu.VMEM((2, 384, elems), BF),
            pltpu.VMEM((6, 160, elems), BF),
            pltpu.VMEM((4, elems, slots), BF),
            pltpu.VMEM((4, 80, slots), F32),
            pltpu.VMEM((4, 80, slots), F32),
            pltpu.VMEM((6, 80, elems), F32),
            pltpu.VMEM((2, 512, elems), BF),
            pltpu.VMEM((2, 320, 384), BF),
            pltpu.VMEM((2, 320, 512), BF),
            pltpu.VMEM((3, 8, width), F32),
            pltpu.VMEM((2, 8, width), F32),
            pltpu.SemaphoreType.DMA((6,)),
            pltpu.SemaphoreType.DMA((6,)),
            pltpu.SemaphoreType.DMA((INPUTS + 5,)),
        ],
        compiler_params=pltpu.CompilerParams(
            collective_id=0, has_side_effects=True, vmem_limit_bytes=60 * 1024 * 1024
        ),
    )(*operands)
    return out, grad


def solution(mesh):
    placed = (
        P(None, None, ("sector", "axial")),
        P(None, None, ("sector", "axial")),
        P(("sector", "axial")),
        P(("sector", "axial")),
        P(),
        P(),
        P(),
        P(None, ("sector", "axial")),
        P(None, ("sector", "axial")),
        P(None, ("sector", "axial")),
        P("sector", "axial", None),
        P(("sector", "axial")),
    )
    return jax.shard_map(
        functools.partial(on_device, mesh.shape["sector"], mesh.shape["axial"]),
        mesh=mesh,
        in_specs=placed,
        out_specs=(P(None, None, ("sector", "axial")), P(("sector", "axial"))),
        check_vma=False,
    )
```

```python
import functools

import jax
import jax.numpy as jnp
import numpy as np
from jax import lax
from jax.experimental import pallas as pl
from jax.experimental.pallas import tpu as pltpu
from jax.sharding import PartitionSpec as P

BLOCKS = 4096
BF = jnp.bfloat16
F32 = jnp.float32
MESH = pl.DeviceIdType.MESH
INPUTS = 15


def lobatto_tables():
    points = np.array([-1.0, -1.0 / np.sqrt(5.0), 1.0 / np.sqrt(5.0), 1.0])
    weights = np.array([1.0, 5.0, 5.0, 1.0]) / 6.0
    scales = np.array(
        [np.prod([points[i] - points[k] for k in range(4) if k != i]) for i in range(4)]
    )
    derivative = np.zeros((4, 4))
    for i in range(4):
        for p in range(4):
            if i != p:
                derivative[i, p] = scales[i] / scales[p] / (points[i] - points[p])
            else:
                derivative[i, p] = sum((1.0 / (points[i] - points[k]) for k in range(4) if k != i))
    node_weight = (
        weights[:, None, None] * weights[None, :, None] * weights[None, None, :]
    ).reshape(64) / 8.0
    return (derivative, node_weight)


def constant_tables():
    derivative, node_weight = lobatto_tables()
    eye = np.eye(4)
    step = derivative.T
    along = [
        np.kron(np.kron(step, eye), eye),
        np.kron(np.kron(eye, step), eye),
        np.kron(np.kron(eye, eye), step),
    ]
    nodes = np.arange(64).reshape(4, 4, 4)
    faces = [nodes[0], nodes[3], nodes[:, 0], nodes[:, 3], nodes[:, :, 0], nodes[:, :, 3]]
    faces = [f.reshape(16) for f in faces]
    mats = list(along)
    pick = np.zeros((96, 64))
    lift = np.zeros((64, 512))
    for f, ids in enumerate(faces):
        diag = np.zeros((64, 64))
        diag[ids, ids] = 1.0
        mats.append(diag)
        pick[16 * f + np.arange(16), ids] = 1.0
        for h in range(5):
            lift[ids, 80 * f + 16 * h + np.arange(16)] = 0.1
    mats = [0.1 * np.concatenate([m, m], axis=1) for m in mats]
    mats.append(np.repeat(node_weight[:, None], 128, axis=1))
    return (
        jnp.asarray(np.stack(mats), F32),
        jnp.asarray(pick, BF),
        jnp.asarray(lift, F32),
    )


def split2(x):
    hi = x.astype(BF)
    return hi, (x - hi.astype(F32)).astype(BF)


def dot(a, b):
    return jnp.dot(a, b, preferred_element_type=F32)


def dot_nt(a, b):
    return lax.dot_general(a, b, (((1,), (1,)), ((), ())), preferred_element_type=F32)


def one_hot(mask):
    return jnp.where(mask, 1.0, 0.0).astype(BF)


def kernel(
    sectors,
    slabs,
    owned,
    *refs,
):
    hbm_refs = refs[:INPUTS]
    out_ref, grad_ref = refs[INPUTS : INPUTS + 2]
    vmem_refs = refs[INPUTS + 2 : 2 * INPUTS + 2]
    rest_refs = refs[2 * INPUTS + 2 :]
    (
        x_ref,
        vel_ref,
        drag_ref,
        bw_ref,
        jac_ref,
        own_ref,
        nbrmat_ref,
        nbr_ref,
        sslots_ref,
        aslots_ref,
        live_ref,
        eb_ref,
        mats_ref,
        pick_ref,
        lift_ref,
    ) = vmem_refs
    (
        xs_ref,
        tr_ref,
        oh_ref,
        send_ref,
        recv_ref,
        part_ref,
        ps_ref,
        a_ref,
        b_ref,
        bsend_ref,
        brecv_ref,
        send_sem,
        recv_sem,
        load_sem,
    ) = rest_refs
    loads = {
        k: pltpu.make_async_copy(hbm_refs[k], vmem_refs[k], load_sem.at[k])
        for k in range(1, INPUTS)
    }
    fields = [
        pltpu.make_async_copy(hbm_refs[0].at[h], x_ref.at[h], load_sem.at[INPUTS + h])
        for h in range(5)
    ]
    for k in (13, 8, 9):
        loads[k].start()
    for field in fields:
        field.start()
    for k in (1, 2, 3, 11, 12, 4, 5, 6, 14, 7, 10):
        loads[k].start()
    elems = x_ref.shape[2]
    slots = sslots_ref.shape[1]
    width = bsend_ref.shape[2]
    count = sectors * slabs
    sec = lax.axis_index("sector")
    axi = lax.axis_index("axial")
    joint = sec * slabs + axi
    prev = lax.rem(joint + count - 1, count)
    nxt = lax.rem(joint + 1, count)
    dev_prev = (prev // slabs, lax.rem(prev, slabs))
    dev_next = (nxt // slabs, lax.rem(nxt, slabs))
    dev_low = (lax.rem(sec + sectors - 1, sectors), axi)
    dev_high = (lax.rem(sec + 1, sectors), axi)

    barrier = pltpu.get_barrier_semaphore()
    for device in (dev_prev, dev_next, dev_low, dev_high):
        pl.semaphore_signal(barrier, inc=1, device_id=device, device_id_type=MESH)

    loads[13].wait()
    for h in range(5):
        fields[h].wait()
        hi, lo = split2(x_ref[h])
        xs_ref[0, 64 * h : 64 * h + 64, :] = hi
        xs_ref[1, 64 * h : 64 * h + 64, :] = lo
        for s, half in enumerate((hi, lo)):
            picked = dot(pick_ref[...], half).astype(BF)
            for f in range(6):
                row = 80 * s + 16 * h
                tr_ref[f, row : row + 16, :] = picked[16 * f : 16 * f + 16, :]
    xs_ref[0, 320:384, :] = jnp.zeros((64, elems), BF)
    xs_ref[1, 320:384, :] = jnp.zeros((64, elems), BF)

    loads[8].wait()
    loads[9].wait()
    rows_slots = lax.broadcasted_iota(jnp.int32, (elems, slots), 0)
    sides = ((0, sslots_ref, 0), (1, sslots_ref, 1), (4, aslots_ref, 0), (5, aslots_ref, 1))
    for i, (face, ref, row) in enumerate(sides):
        hot = one_hot(rows_slots == ref[row : row + 1, :])
        oh_ref[i] = hot
        both = dot(tr_ref[face], hot)
        send_ref[i] = both[:80] + both[80:]

    pl.semaphore_wait(barrier, 4)

    def remote(src, dst, k, device):
        return pltpu.make_async_remote_copy(
            src_ref=src,
            dst_ref=dst,
            send_sem=send_sem.at[k],
            recv_sem=recv_sem.at[k],
            device_id=device,
            device_id_type=MESH,
        )

    up_x = remote(send_ref.at[1], recv_ref.at[0], 0, dev_high)
    down_x = remote(send_ref.at[0], recv_ref.at[1], 1, dev_low)
    up_z = remote(send_ref.at[3], recv_ref.at[2], 2, dev_next)
    down_z = remote(send_ref.at[2], recv_ref.at[3], 3, dev_prev)
    up_b = remote(bsend_ref.at[2], brecv_ref.at[0], 4, dev_next)
    down_b = remote(bsend_ref.at[0], brecv_ref.at[1], 5, dev_prev)
    has_low = axi > 0
    has_high = axi < slabs - 1
    up_x.start()
    down_x.start()

    @pl.when(has_high)
    def _():
        up_z.start()

    @pl.when(has_low)
    def _():
        down_z.start()

    @pl.when(jnp.logical_not(has_low))
    def _():
        recv_ref[2] = jnp.zeros((80, slots), F32)

    @pl.when(jnp.logical_not(has_high))
    def _():
        recv_ref[3] = jnp.zeros((80, slots), F32)

    for k in (1, 2, 3, 11, 12):
        loads[k].wait()
    drag = drag_ref[...]
    acc = x_ref[1] * vel_ref[0].astype(F32)
    acc += x_ref[2] * vel_ref[1].astype(F32)
    acc += x_ref[3] * vel_ref[2].astype(F32)
    elem_grad = drag * jnp.sum(acc * mats_ref[9][:, 0:1], axis=0, keepdims=True)
    weighted = bw_ref[...] * elem_grad
    w1 = weighted.astype(BF)
    rest = weighted - w1.astype(F32)
    w2 = rest.astype(BF)
    w3 = (rest - w2.astype(F32)).astype(BF).astype(F32)
    row16 = lax.broadcasted_iota(jnp.int32, (16, elems), 0)
    stack = jnp.where(row16 == 0, w1.astype(F32), 0.0)
    stack = jnp.where(row16 == 1, w2.astype(F32), stack)
    stack = jnp.where(row16 == 2, w3, stack).astype(BF)
    rel = eb_ref[...] - (joint - 1) * owned
    rel = jnp.where(rel < 0, rel + BLOCKS, rel)
    rel = jnp.where(rel >= BLOCKS, rel - BLOCKS, rel)
    rows_blk = lax.broadcasted_iota(jnp.int32, (width, elems), 0)
    for j in range(3):
        sums = dot_nt(stack, one_hot(rows_blk == rel - j * owned))
        total = jnp.sum(sums, axis=0, keepdims=True)
        bsend_ref[j] = jnp.broadcast_to(total, (8, width))
    up_b.start()
    down_b.start()

    for k in (4, 5, 6, 14):
        loads[k].wait()
    spread = lax.broadcasted_iota(jnp.int32, (5, 384), 1) // 64
    spread = jnp.where(spread == lax.broadcasted_iota(jnp.int32, (5, 384), 0), 1.0, 0.0)
    lane = lax.broadcasted_iota(jnp.int32, (6, 512), 1)
    face_row = lax.broadcasted_iota(jnp.int32, (6, 512), 0)
    slot_row = lane // 16 - 5 * face_row
    for c in range(5):
        rows = slice(64 * c, 64 * c + 64)
        jac = jac_ref[0][:, c : c + 1] * spread[0:1, :]
        face = own_ref[c][:, 0:1] * spread[0:1, :]
        nbrs = jnp.where(slot_row == 0, nbrmat_ref[c][:, 0:1], 0.0)
        for h in range(1, 5):
            jac += jac_ref[h][:, c : c + 1] * spread[h : h + 1, :]
            face += own_ref[c][:, h : h + 1] * spread[h : h + 1, :]
            nbrs = jnp.where(slot_row == h, nbrmat_ref[c][:, h : h + 1], nbrs)
        rown = jnp.sum(nbrs, axis=0, keepdims=True)
        for t in range(3):
            lanes = slice(128 * t, 128 * t + 128)
            total = mats_ref[0] * jac[0:1, lanes]
            for j in range(1, 9):
                row = jac[j : j + 1, lanes] if j < 3 else face[j - 3 : j - 2, lanes]
                total += mats_ref[j] * row
            a_ref[0, rows, lanes], a_ref[1, rows, lanes] = split2(total)
        b_ref[0, rows, :], b_ref[1, rows, :] = split2(lift_ref[...] * rown)

    own = dot(a_ref[0], xs_ref[0]) + dot(a_ref[0], xs_ref[1]) + dot(a_ref[1], xs_ref[0])
    keep = 1.0 - 0.1 * drag
    for c in range(5):
        x = x_ref[c]
        scaled = x * keep if 1 <= c <= 3 else x
        out_ref[c] = scaled + own[64 * c : 64 * c + 64, :]

    loads[7].wait()
    chunk = 256
    rows_src = lax.broadcasted_iota(jnp.int32, (chunk, elems), 0)

    def gather(f, carry):
        ids = nbr_ref[pl.ds(f, 1), :]
        g = f + 1 - 2 * lax.rem(f, 2)
        both = jnp.zeros((160, elems), F32)
        for k in range(elems // chunk):
            hot = one_hot(rows_src == ids - k * chunk)
            both += dot(tr_ref[g, :, k * chunk : (k + 1) * chunk], hot)
        part_ref[f] = both[:80] + both[80:]
        return carry

    lax.fori_loop(0, 6, gather, 0)

    up_x.wait()
    down_x.wait()

    @pl.when(has_high)
    def _():
        up_z.wait_send()
        down_z.wait_recv()

    @pl.when(has_low)
    def _():
        down_z.wait_send()
        up_z.wait_recv()

    loads[10].wait()
    slot_ids = lax.broadcasted_iota(jnp.int32, (80, slots), 1)
    for i, face in enumerate((0, 1, 4, 5)):
        got = recv_ref[i]
        if i < 2:
            got = jnp.where(slot_ids < live_ref[:, i : i + 1], got, 0.0)
        both = dot_nt(jnp.concatenate(split2(got), axis=0), oh_ref[i])
        part_ref[face] += both[:80] + both[80:]
    for f in range(6):
        rows = slice(80 * f, 80 * f + 80)
        ps_ref[0, rows, :], ps_ref[1, rows, :] = split2(part_ref[f])
    for s in range(2):
        ps_ref[s, 480:512, :] = jnp.zeros((32, elems), BF)
    nbr = dot(b_ref[0], ps_ref[0]) + dot(b_ref[0], ps_ref[1]) + dot(b_ref[1], ps_ref[0])
    for c in range(5):
        out_ref[c] += nbr[64 * c : 64 * c + 64, :]

    up_b.wait()
    down_b.wait()
    sums = bsend_ref[1] + brecv_ref[0] + brecv_ref[1]
    grad_ref[...] = sums[0, :owned]


def on_device(
    sectors,
    slabs,
    adjoint,
    velocity,
    drag,
    block_weight,
    flux_jac,
    face_own,
    face_nbr,
    nbr_local,
    sector_slots,
    axial_slots,
    sector_live,
    elem_block,
):
    elems = adjoint.shape[2]
    slots = sector_slots.shape[1]
    owned = BLOCKS // (sectors * slabs)
    width = -(-owned // 128) * 128
    operands = (
        adjoint,
        velocity,
        drag.reshape(1, elems),
        block_weight.reshape(1, elems),
        jnp.transpose(flux_jac, (1, 0, 2)),
        jnp.transpose(face_own, (1, 0, 2)),
        jnp.transpose(face_nbr, (1, 0, 2)),
        nbr_local,
        sector_slots,
        axial_slots,
        sector_live.reshape(1, 2),
        elem_block.reshape(1, elems),
        *constant_tables(),
    )
    vmem = pl.BlockSpec(memory_space=pltpu.VMEM)
    hbm = pl.BlockSpec(memory_space=pltpu.HBM)
    out, grad = pl.pallas_call(
        functools.partial(kernel, sectors, slabs, owned),
        out_shape=(
            pltpu.VMEM(adjoint.shape, F32),
            pltpu.VMEM((owned,), F32),
        ),
        in_specs=[hbm] * INPUTS,
        out_specs=(vmem, vmem),
        scratch_shapes=[pltpu.VMEM(a.shape, a.dtype) for a in operands]
        + [
            pltpu.VMEM((2, 384, elems), BF),
            pltpu.VMEM((6, 160, elems), BF),
            pltpu.VMEM((4, elems, slots), BF),
            pltpu.VMEM((4, 80, slots), F32),
            pltpu.VMEM((4, 80, slots), F32),
            pltpu.VMEM((6, 80, elems), F32),
            pltpu.VMEM((2, 512, elems), BF),
            pltpu.VMEM((2, 320, 384), BF),
            pltpu.VMEM((2, 320, 512), BF),
            pltpu.VMEM((3, 8, width), F32),
            pltpu.VMEM((2, 8, width), F32),
            pltpu.SemaphoreType.DMA((6,)),
            pltpu.SemaphoreType.DMA((6,)),
            pltpu.SemaphoreType.DMA((INPUTS + 5,)),
        ],
        compiler_params=pltpu.CompilerParams(
            collective_id=0, has_side_effects=True, vmem_limit_bytes=60 * 1024 * 1024
        ),
    )(*operands)
    return out, grad


def solution(mesh):
    placed = (
        P(None, None, ("sector", "axial")),
        P(None, None, ("sector", "axial")),
        P(("sector", "axial")),
        P(("sector", "axial")),
        P(),
        P(),
        P(),
        P(None, ("sector", "axial")),
        P(None, ("sector", "axial")),
        P(None, ("sector", "axial")),
        P("sector", "axial", None),
        P(("sector", "axial")),
    )
    return jax.shard_map(
        functools.partial(on_device, mesh.shape["sector"], mesh.shape["axial"]),
        mesh=mesh,
        in_specs=placed,
        out_specs=(P(None, None, ("sector", "axial")), P(("sector", "axial"))),
        check_vma=False,
    )
```

```python
import functools

import jax
import jax.numpy as jnp
import numpy as np
from jax import lax
from jax.experimental import pallas as pl
from jax.experimental.pallas import tpu as pltpu
from jax.sharding import PartitionSpec as P

BLOCKS = 4096
BF = jnp.bfloat16
F32 = jnp.float32
MESH = pl.DeviceIdType.MESH
INPUTS = 15


def lobatto_tables():
    points = np.array([-1.0, -1.0 / np.sqrt(5.0), 1.0 / np.sqrt(5.0), 1.0])
    weights = np.array([1.0, 5.0, 5.0, 1.0]) / 6.0
    scales = np.array(
        [np.prod([points[i] - points[k] for k in range(4) if k != i]) for i in range(4)]
    )
    derivative = np.zeros((4, 4))
    for i in range(4):
        for p in range(4):
            if i != p:
                derivative[i, p] = scales[i] / scales[p] / (points[i] - points[p])
            else:
                derivative[i, p] = sum((1.0 / (points[i] - points[k]) for k in range(4) if k != i))
    node_weight = (
        weights[:, None, None] * weights[None, :, None] * weights[None, None, :]
    ).reshape(64) / 8.0
    return (derivative, node_weight)


def constant_tables():
    derivative, node_weight = lobatto_tables()
    eye = np.eye(4)
    step = derivative.T
    along = [
        np.kron(np.kron(step, eye), eye),
        np.kron(np.kron(eye, step), eye),
        np.kron(np.kron(eye, eye), step),
    ]
    nodes = np.arange(64).reshape(4, 4, 4)
    faces = [nodes[0], nodes[3], nodes[:, 0], nodes[:, 3], nodes[:, :, 0], nodes[:, :, 3]]
    faces = [f.reshape(16) for f in faces]
    mats = list(along)
    pick = np.zeros((96, 64))
    lift = np.zeros((64, 512))
    for f, ids in enumerate(faces):
        diag = np.zeros((64, 64))
        diag[ids, ids] = 1.0
        mats.append(diag)
        pick[16 * f + np.arange(16), ids] = 1.0
        for h in range(5):
            lift[ids, 80 * f + 16 * h + np.arange(16)] = 0.1
    mats = [0.1 * np.concatenate([m, m], axis=1) for m in mats]
    mats.append(np.repeat(node_weight[:, None], 128, axis=1))
    return (
        jnp.asarray(np.stack(mats), F32),
        jnp.asarray(pick, BF),
        jnp.asarray(lift, F32),
    )


def split2(x):
    hi = x.astype(BF)
    return hi, (x - hi.astype(F32)).astype(BF)


def dot(a, b):
    return jnp.dot(a, b, preferred_element_type=F32)


def dot_nt(a, b):
    return lax.dot_general(a, b, (((1,), (1,)), ((), ())), preferred_element_type=F32)


def one_hot(mask):
    return jnp.where(mask, 1.0, 0.0).astype(BF)


def kernel(
    sectors,
    slabs,
    owned,
    *refs,
):
    hbm_refs = refs[:INPUTS]
    out_ref, grad_ref = refs[INPUTS : INPUTS + 2]
    vmem_refs = refs[INPUTS + 2 : 2 * INPUTS + 2]
    rest_refs = refs[2 * INPUTS + 2 :]
    (
        x_ref,
        vel_ref,
        drag_ref,
        bw_ref,
        jac_ref,
        own_ref,
        nbrmat_ref,
        nbr_ref,
        sslots_ref,
        aslots_ref,
        live_ref,
        eb_ref,
        mats_ref,
        pick_ref,
        lift_ref,
    ) = vmem_refs
    (
        xs_ref,
        tr_ref,
        oh_ref,
        send_ref,
        recv_ref,
        part_ref,
        ps_ref,
        a_ref,
        b_ref,
        bsend_ref,
        brecv_ref,
        send_sem,
        recv_sem,
        load_sem,
    ) = rest_refs
    loads = {
        k: pltpu.make_async_copy(hbm_refs[k], vmem_refs[k], load_sem.at[k])
        for k in range(1, INPUTS)
    }
    fields = [
        pltpu.make_async_copy(hbm_refs[0].at[h], x_ref.at[h], load_sem.at[INPUTS + h])
        for h in range(5)
    ]
    for k in (8, 9, 4, 5, 6, 12, 14, 13):
        loads[k].start()
    for field in fields:
        field.start()
    for k in (1, 2, 3, 11, 7, 10):
        loads[k].start()
    elems = x_ref.shape[2]
    slots = sslots_ref.shape[1]
    width = bsend_ref.shape[2]
    count = sectors * slabs
    sec = lax.axis_index("sector")
    axi = lax.axis_index("axial")
    joint = sec * slabs + axi
    prev = lax.rem(joint + count - 1, count)
    nxt = lax.rem(joint + 1, count)
    dev_prev = (prev // slabs, lax.rem(prev, slabs))
    dev_next = (nxt // slabs, lax.rem(nxt, slabs))
    dev_low = (lax.rem(sec + sectors - 1, sectors), axi)
    dev_high = (lax.rem(sec + 1, sectors), axi)

    barrier = pltpu.get_barrier_semaphore()
    for device in (dev_prev, dev_next, dev_low, dev_high):
        pl.semaphore_signal(barrier, inc=1, device_id=device, device_id_type=MESH)

    loads[8].wait()
    loads[9].wait()
    rows_slots = lax.broadcasted_iota(jnp.int32, (elems, slots), 0)
    sides = ((0, sslots_ref, 0), (1, sslots_ref, 1), (4, aslots_ref, 0), (5, aslots_ref, 1))
    for i, (face, ref, row) in enumerate(sides):
        oh_ref[i] = one_hot(rows_slots == ref[row : row + 1, :])

    for k in (4, 5, 6, 12, 14):
        loads[k].wait()
    spread = lax.broadcasted_iota(jnp.int32, (5, 384), 1) // 64
    spread = jnp.where(spread == lax.broadcasted_iota(jnp.int32, (5, 384), 0), 1.0, 0.0)
    lane = lax.broadcasted_iota(jnp.int32, (6, 512), 1)
    face_row = lax.broadcasted_iota(jnp.int32, (6, 512), 0)
    slot_row = lane // 16 - 5 * face_row
    for c in range(5):
        rows = slice(64 * c, 64 * c + 64)
        jac = jac_ref[0][:, c : c + 1] * spread[0:1, :]
        face = own_ref[c][:, 0:1] * spread[0:1, :]
        nbrs = jnp.where(slot_row == 0, nbrmat_ref[c][:, 0:1], 0.0)
        for h in range(1, 5):
            jac += jac_ref[h][:, c : c + 1] * spread[h : h + 1, :]
            face += own_ref[c][:, h : h + 1] * spread[h : h + 1, :]
            nbrs = jnp.where(slot_row == h, nbrmat_ref[c][:, h : h + 1], nbrs)
        rown = jnp.sum(nbrs, axis=0, keepdims=True)
        for t in range(3):
            lanes = slice(128 * t, 128 * t + 128)
            total = mats_ref[0] * jac[0:1, lanes]
            for j in range(1, 9):
                row = jac[j : j + 1, lanes] if j < 3 else face[j - 3 : j - 2, lanes]
                total += mats_ref[j] * row
            hi, lo = split2(total)
            for base, part in ((0, hi), (384, hi), (768, lo)):
                a_ref[rows, base + 128 * t : base + 128 * t + 128] = part
        hi, lo = split2(lift_ref[...] * rown)
        b_ref[rows, 0:512] = hi
        b_ref[rows, 512:1024] = hi
        b_ref[rows, 1024:1536] = lo

    loads[13].wait()
    for h in range(5):
        fields[h].wait()
        hi, lo = split2(x_ref[h])
        for base, part in ((0, hi), (384, lo), (768, hi)):
            xs_ref[base + 64 * h : base + 64 * h + 64, :] = part
        for s, half in enumerate((hi, lo)):
            picked = dot(pick_ref[...], half).astype(BF)
            for f in range(6):
                row = 80 * s + 16 * h
                tr_ref[f, row : row + 16, :] = picked[16 * f : 16 * f + 16, :]
    for base in (320, 704, 1088):
        xs_ref[base : base + 64, :] = jnp.zeros((64, elems), BF)

    for i, face in enumerate((0, 1, 4, 5)):
        both = dot(tr_ref[face], oh_ref[i])
        send_ref[i] = both[:80] + both[80:]

    pl.semaphore_wait(barrier, 4)

    def remote(src, dst, k, device):
        return pltpu.make_async_remote_copy(
            src_ref=src,
            dst_ref=dst,
            send_sem=send_sem.at[k],
            recv_sem=recv_sem.at[k],
            device_id=device,
            device_id_type=MESH,
        )

    up_x = remote(send_ref.at[1], recv_ref.at[0], 0, dev_high)
    down_x = remote(send_ref.at[0], recv_ref.at[1], 1, dev_low)
    up_z = remote(send_ref.at[3], recv_ref.at[2], 2, dev_next)
    down_z = remote(send_ref.at[2], recv_ref.at[3], 3, dev_prev)
    up_b = remote(bsend_ref.at[2], brecv_ref.at[0], 4, dev_next)
    down_b = remote(bsend_ref.at[0], brecv_ref.at[1], 5, dev_prev)
    has_low = axi > 0
    has_high = axi < slabs - 1
    up_x.start()
    down_x.start()

    @pl.when(has_high)
    def _():
        up_z.start()

    @pl.when(has_low)
    def _():
        down_z.start()

    @pl.when(jnp.logical_not(has_low))
    def _():
        recv_ref[2] = jnp.zeros((80, slots), F32)

    @pl.when(jnp.logical_not(has_high))
    def _():
        recv_ref[3] = jnp.zeros((80, slots), F32)

    for k in (1, 2, 3, 11):
        loads[k].wait()
    drag = drag_ref[...]
    acc = x_ref[1] * vel_ref[0].astype(F32)
    acc += x_ref[2] * vel_ref[1].astype(F32)
    acc += x_ref[3] * vel_ref[2].astype(F32)
    elem_grad = drag * jnp.sum(acc * mats_ref[9][:, 0:1], axis=0, keepdims=True)
    weighted = bw_ref[...] * elem_grad
    w1 = weighted.astype(BF)
    rest = weighted - w1.astype(F32)
    w2 = rest.astype(BF)
    w3 = (rest - w2.astype(F32)).astype(BF).astype(F32)
    row16 = lax.broadcasted_iota(jnp.int32, (16, elems), 0)
    stack = jnp.where(row16 == 0, w1.astype(F32), 0.0)
    stack = jnp.where(row16 == 1, w2.astype(F32), stack)
    stack = jnp.where(row16 == 2, w3, stack).astype(BF)
    rel = eb_ref[...] - (joint - 1) * owned
    rel = jnp.where(rel < 0, rel + BLOCKS, rel)
    rel = jnp.where(rel >= BLOCKS, rel - BLOCKS, rel)
    rows_blk = lax.broadcasted_iota(jnp.int32, (width, elems), 0)
    for j in range(3):
        sums = dot_nt(stack, one_hot(rows_blk == rel - j * owned))
        total = jnp.sum(sums, axis=0, keepdims=True)
        bsend_ref[j] = jnp.broadcast_to(total, (8, width))
    up_b.start()
    down_b.start()

    own = dot(a_ref[...], xs_ref[...])
    keep = 1.0 - 0.1 * drag
    for c in range(5):
        x = x_ref[c]
        scaled = x * keep if 1 <= c <= 3 else x
        out_ref[c] = scaled + own[64 * c : 64 * c + 64, :]

    loads[7].wait()
    chunk = 256
    rows_src = lax.broadcasted_iota(jnp.int32, (chunk, elems), 0)

    def gather(f, carry):
        ids = nbr_ref[pl.ds(f, 1), :]
        g = f + 1 - 2 * lax.rem(f, 2)
        both = jnp.zeros((160, elems), F32)
        for k in range(elems // chunk):
            hot = one_hot(rows_src == ids - k * chunk)
            both += dot(tr_ref[g, :, k * chunk : (k + 1) * chunk], hot)
        part_ref[f] = both[:80] + both[80:]
        return carry

    lax.fori_loop(0, 6, gather, 0)

    def put_partner(face, value):
        hi, lo = split2(value)
        for base, part in ((0, hi), (512, lo), (1024, hi)):
            ps_ref[base + 80 * face : base + 80 * face + 80, :] = part

    put_partner(2, part_ref[2])
    put_partner(3, part_ref[3])
    for base in (480, 992, 1504):
        ps_ref[base : base + 32, :] = jnp.zeros((32, elems), BF)

    up_x.wait()
    down_x.wait()

    @pl.when(has_high)
    def _():
        up_z.wait_send()
        down_z.wait_recv()

    @pl.when(has_low)
    def _():
        down_z.wait_send()
        up_z.wait_recv()

    loads[10].wait()
    slot_ids = lax.broadcasted_iota(jnp.int32, (80, slots), 1)
    for i, face in enumerate((0, 1, 4, 5)):
        got = recv_ref[i]
        if i < 2:
            got = jnp.where(slot_ids < live_ref[:, i : i + 1], got, 0.0)
        both = dot_nt(jnp.concatenate(split2(got), axis=0), oh_ref[i])
        put_partner(face, part_ref[face] + (both[:80] + both[80:]))
    nbr = dot(b_ref[...], ps_ref[...])
    for c in range(5):
        out_ref[c] += nbr[64 * c : 64 * c + 64, :]

    up_b.wait()
    down_b.wait()
    sums = bsend_ref[1] + brecv_ref[0] + brecv_ref[1]
    grad_ref[...] = sums[0, :owned]


def on_device(
    sectors,
    slabs,
    adjoint,
    velocity,
    drag,
    block_weight,
    flux_jac,
    face_own,
    face_nbr,
    nbr_local,
    sector_slots,
    axial_slots,
    sector_live,
    elem_block,
):
    elems = adjoint.shape[2]
    slots = sector_slots.shape[1]
    owned = BLOCKS // (sectors * slabs)
    width = -(-owned // 128) * 128
    operands = (
        adjoint,
        velocity,
        drag.reshape(1, elems),
        block_weight.reshape(1, elems),
        jnp.transpose(flux_jac, (1, 0, 2)),
        jnp.transpose(face_own, (1, 0, 2)),
        jnp.transpose(face_nbr, (1, 0, 2)),
        nbr_local,
        sector_slots,
        axial_slots,
        sector_live.reshape(1, 2),
        elem_block.reshape(1, elems),
        *constant_tables(),
    )
    vmem = pl.BlockSpec(memory_space=pltpu.VMEM)
    hbm = pl.BlockSpec(memory_space=pltpu.HBM)
    out, grad = pl.pallas_call(
        functools.partial(kernel, sectors, slabs, owned),
        out_shape=(
            pltpu.VMEM(adjoint.shape, F32),
            pltpu.VMEM((owned,), F32),
        ),
        in_specs=[hbm] * INPUTS,
        out_specs=(vmem, vmem),
        scratch_shapes=[pltpu.VMEM(a.shape, a.dtype) for a in operands]
        + [
            pltpu.VMEM((1152, elems), BF),
            pltpu.VMEM((6, 160, elems), BF),
            pltpu.VMEM((4, elems, slots), BF),
            pltpu.VMEM((4, 80, slots), F32),
            pltpu.VMEM((4, 80, slots), F32),
            pltpu.VMEM((6, 80, elems), F32),
            pltpu.VMEM((1536, elems), BF),
            pltpu.VMEM((320, 1152), BF),
            pltpu.VMEM((320, 1536), BF),
            pltpu.VMEM((3, 8, width), F32),
            pltpu.VMEM((2, 8, width), F32),
            pltpu.SemaphoreType.DMA((6,)),
            pltpu.SemaphoreType.DMA((6,)),
            pltpu.SemaphoreType.DMA((INPUTS + 5,)),
        ],
        compiler_params=pltpu.CompilerParams(
            collective_id=0, has_side_effects=True, vmem_limit_bytes=60 * 1024 * 1024
        ),
    )(*operands)
    return out, grad


def solution(mesh):
    placed = (
        P(None, None, ("sector", "axial")),
        P(None, None, ("sector", "axial")),
        P(("sector", "axial")),
        P(("sector", "axial")),
        P(),
        P(),
        P(),
        P(None, ("sector", "axial")),
        P(None, ("sector", "axial")),
        P(None, ("sector", "axial")),
        P("sector", "axial", None),
        P(("sector", "axial")),
    )
    return jax.shard_map(
        functools.partial(on_device, mesh.shape["sector"], mesh.shape["axial"]),
        mesh=mesh,
        in_specs=placed,
        out_specs=(P(None, None, ("sector", "axial")), P(("sector", "axial"))),
        check_vma=False,
    )
```

```python
import functools

import jax
import jax.numpy as jnp
import numpy as np
from jax import lax
from jax.experimental import pallas as pl
from jax.experimental.pallas import tpu as pltpu
from jax.sharding import PartitionSpec as P

BLOCKS = 4096
BF = jnp.bfloat16
F32 = jnp.float32
MESH = pl.DeviceIdType.MESH
INPUTS = 15


def lobatto_tables():
    points = np.array([-1.0, -1.0 / np.sqrt(5.0), 1.0 / np.sqrt(5.0), 1.0])
    weights = np.array([1.0, 5.0, 5.0, 1.0]) / 6.0
    scales = np.array(
        [np.prod([points[i] - points[k] for k in range(4) if k != i]) for i in range(4)]
    )
    derivative = np.zeros((4, 4))
    for i in range(4):
        for p in range(4):
            if i != p:
                derivative[i, p] = scales[i] / scales[p] / (points[i] - points[p])
            else:
                derivative[i, p] = sum((1.0 / (points[i] - points[k]) for k in range(4) if k != i))
    node_weight = (
        weights[:, None, None] * weights[None, :, None] * weights[None, None, :]
    ).reshape(64) / 8.0
    return (derivative, node_weight)


def constant_tables():
    derivative, node_weight = lobatto_tables()
    eye = np.eye(4)
    step = derivative.T
    along = [
        np.kron(np.kron(step, eye), eye),
        np.kron(np.kron(eye, step), eye),
        np.kron(np.kron(eye, eye), step),
    ]
    nodes = np.arange(64).reshape(4, 4, 4)
    faces = [nodes[0], nodes[3], nodes[:, 0], nodes[:, 3], nodes[:, :, 0], nodes[:, :, 3]]
    faces = [f.reshape(16) for f in faces]
    mats = list(along)
    pick = np.zeros((96, 64))
    lift = np.zeros((64, 512))
    for f, ids in enumerate(faces):
        diag = np.zeros((64, 64))
        diag[ids, ids] = 1.0
        mats.append(diag)
        pick[16 * f + np.arange(16), ids] = 1.0
        for h in range(5):
            lift[ids, 80 * f + 16 * h + np.arange(16)] = 0.1
    mats = [0.1 * np.concatenate([m, m], axis=1) for m in mats]
    mats.append(np.repeat(node_weight[:, None], 128, axis=1))
    return (
        jnp.asarray(np.stack(mats), F32),
        jnp.asarray(pick, BF),
        jnp.asarray(lift, F32),
    )


def split2(x):
    hi = x.astype(BF)
    return hi, (x - hi.astype(F32)).astype(BF)


def dot(a, b):
    return jnp.dot(a, b, preferred_element_type=F32)


def dot_nt(a, b):
    return lax.dot_general(a, b, (((1,), (1,)), ((), ())), preferred_element_type=F32)


def one_hot(mask):
    return jnp.where(mask, 1.0, 0.0).astype(BF)


def kernel(
    sectors,
    slabs,
    owned,
    *refs,
):
    hbm_refs = refs[:INPUTS]
    out_ref, grad_ref = refs[INPUTS : INPUTS + 2]
    vmem_refs = refs[INPUTS + 2 : 2 * INPUTS + 2]
    rest_refs = refs[2 * INPUTS + 2 :]
    (
        x_ref,
        vel_ref,
        drag_ref,
        bw_ref,
        jac_ref,
        own_ref,
        nbrmat_ref,
        nbr_ref,
        sslots_ref,
        aslots_ref,
        live_ref,
        eb_ref,
        mats_ref,
        pick_ref,
        lift_ref,
    ) = vmem_refs
    (
        xs_ref,
        tr_ref,
        oh_ref,
        send_ref,
        recv_ref,
        part_ref,
        ps_ref,
        a_ref,
        b_ref,
        bsend_ref,
        brecv_ref,
        send_sem,
        recv_sem,
        load_sem,
    ) = rest_refs
    loads = {
        k: pltpu.make_async_copy(hbm_refs[k], vmem_refs[k], load_sem.at[k])
        for k in range(1, INPUTS)
    }
    fields = [
        pltpu.make_async_copy(hbm_refs[0].at[h], x_ref.at[h], load_sem.at[INPUTS + h])
        for h in range(5)
    ]
    for k in (8, 9, 4, 5, 6, 12, 14, 13):
        loads[k].start()
    for field in fields:
        field.start()
    for k in (1, 2, 3, 11, 7, 10):
        loads[k].start()
    elems = x_ref.shape[2]
    slots = sslots_ref.shape[1]
    width = bsend_ref.shape[2]
    count = sectors * slabs
    sec = lax.axis_index("sector")
    axi = lax.axis_index("axial")
    joint = sec * slabs + axi
    prev = lax.rem(joint + count - 1, count)
    nxt = lax.rem(joint + 1, count)
    dev_prev = (prev // slabs, lax.rem(prev, slabs))
    dev_next = (nxt // slabs, lax.rem(nxt, slabs))
    dev_low = (lax.rem(sec + sectors - 1, sectors), axi)
    dev_high = (lax.rem(sec + 1, sectors), axi)

    barrier = pltpu.get_barrier_semaphore()
    for device in (dev_prev, dev_next, dev_low, dev_high):
        pl.semaphore_signal(barrier, inc=1, device_id=device, device_id_type=MESH)

    loads[8].wait()
    loads[9].wait()
    rows_slots = lax.broadcasted_iota(jnp.int32, (elems, slots), 0)
    sides = ((0, sslots_ref, 0), (1, sslots_ref, 1), (4, aslots_ref, 0), (5, aslots_ref, 1))
    for i, (face, ref, row) in enumerate(sides):
        oh_ref[i] = one_hot(rows_slots == ref[row : row + 1, :])

    for k in (4, 5, 6, 12, 14):
        loads[k].wait()
    spread = lax.broadcasted_iota(jnp.int32, (5, 384), 1) // 64
    spread = jnp.where(spread == lax.broadcasted_iota(jnp.int32, (5, 384), 0), 1.0, 0.0)
    lane = lax.broadcasted_iota(jnp.int32, (6, 512), 1)
    face_row = lax.broadcasted_iota(jnp.int32, (6, 512), 0)
    slot_row = lane // 16 - 5 * face_row
    for c in range(5):
        rows = slice(64 * c, 64 * c + 64)
        jac = jac_ref[0][:, c : c + 1] * spread[0:1, :]
        face = own_ref[c][:, 0:1] * spread[0:1, :]
        nbrs = jnp.where(slot_row == 0, nbrmat_ref[c][:, 0:1], 0.0)
        for h in range(1, 5):
            jac += jac_ref[h][:, c : c + 1] * spread[h : h + 1, :]
            face += own_ref[c][:, h : h + 1] * spread[h : h + 1, :]
            nbrs = jnp.where(slot_row == h, nbrmat_ref[c][:, h : h + 1], nbrs)
        rown = jnp.sum(nbrs, axis=0, keepdims=True)
        for t in range(3):
            lanes = slice(128 * t, 128 * t + 128)
            total = mats_ref[0] * jac[0:1, lanes]
            for j in range(1, 9):
                row = jac[j : j + 1, lanes] if j < 3 else face[j - 3 : j - 2, lanes]
                total += mats_ref[j] * row
            hi, lo = split2(total)
            for base, part in ((0, hi), (384, hi), (768, lo)):
                a_ref[rows, base + 128 * t : base + 128 * t + 128] = part
        hi, lo = split2(lift_ref[...] * rown)
        b_ref[rows, 0:512] = hi
        b_ref[rows, 512:1024] = hi
        b_ref[rows, 1024:1536] = lo

    loads[13].wait()
    for field in fields:
        field.wait()

    def trace(h, carry):
        hi, lo = split2(x_ref[h])
        for base, part in ((0, hi), (384, lo), (768, hi)):
            xs_ref[pl.ds(pl.multiple_of(base + 64 * h, 64), 64), :] = part
        for s, half in enumerate((hi, lo)):
            picked = dot(pick_ref[...], half).astype(BF)
            for f in range(6):
                row = pl.multiple_of(80 * s + 16 * h, 16)
                tr_ref[f, pl.ds(row, 16), :] = picked[16 * f : 16 * f + 16, :]
        return carry

    lax.fori_loop(0, 5, trace, 0)
    for base in (320, 704, 1088):
        xs_ref[base : base + 64, :] = jnp.zeros((64, elems), BF)

    for i, face in enumerate((0, 1, 4, 5)):
        both = dot(tr_ref[face], oh_ref[i])
        send_ref[i] = both[:80] + both[80:]

    pl.semaphore_wait(barrier, 4)

    def remote(src, dst, k, device):
        return pltpu.make_async_remote_copy(
            src_ref=src,
            dst_ref=dst,
            send_sem=send_sem.at[k],
            recv_sem=recv_sem.at[k],
            device_id=device,
            device_id_type=MESH,
        )

    up_x = remote(send_ref.at[1], recv_ref.at[0], 0, dev_high)
    down_x = remote(send_ref.at[0], recv_ref.at[1], 1, dev_low)
    up_z = remote(send_ref.at[3], recv_ref.at[2], 2, dev_next)
    down_z = remote(send_ref.at[2], recv_ref.at[3], 3, dev_prev)
    up_b = remote(bsend_ref.at[2], brecv_ref.at[0], 4, dev_next)
    down_b = remote(bsend_ref.at[0], brecv_ref.at[1], 5, dev_prev)
    has_low = axi > 0
    has_high = axi < slabs - 1
    up_x.start()
    down_x.start()

    @pl.when(has_high)
    def _():
        up_z.start()

    @pl.when(has_low)
    def _():
        down_z.start()

    @pl.when(jnp.logical_not(has_low))
    def _():
        recv_ref[2] = jnp.zeros((80, slots), F32)

    @pl.when(jnp.logical_not(has_high))
    def _():
        recv_ref[3] = jnp.zeros((80, slots), F32)

    for k in (1, 2, 3, 11):
        loads[k].wait()
    drag = drag_ref[...]
    acc = x_ref[1] * vel_ref[0].astype(F32)
    acc += x_ref[2] * vel_ref[1].astype(F32)
    acc += x_ref[3] * vel_ref[2].astype(F32)
    elem_grad = drag * jnp.sum(acc * mats_ref[9][:, 0:1], axis=0, keepdims=True)
    weighted = bw_ref[...] * elem_grad
    w1 = weighted.astype(BF)
    rest = weighted - w1.astype(F32)
    w2 = rest.astype(BF)
    w3 = (rest - w2.astype(F32)).astype(BF).astype(F32)
    row16 = lax.broadcasted_iota(jnp.int32, (16, elems), 0)
    stack = jnp.where(row16 == 0, w1.astype(F32), 0.0)
    stack = jnp.where(row16 == 1, w2.astype(F32), stack)
    stack = jnp.where(row16 == 2, w3, stack).astype(BF)
    rel = eb_ref[...] - (joint - 1) * owned
    rel = jnp.where(rel < 0, rel + BLOCKS, rel)
    rel = jnp.where(rel >= BLOCKS, rel - BLOCKS, rel)
    rows_blk = lax.broadcasted_iota(jnp.int32, (width, elems), 0)
    for j in range(3):
        sums = dot_nt(stack, one_hot(rows_blk == rel - j * owned))
        total = jnp.sum(sums, axis=0, keepdims=True)
        bsend_ref[j] = jnp.broadcast_to(total, (8, width))
    up_b.start()
    down_b.start()

    own = dot(a_ref[...], xs_ref[...])
    keep = 1.0 - 0.1 * drag
    for c in range(5):
        x = x_ref[c]
        scaled = x * keep if 1 <= c <= 3 else x
        out_ref[c] = scaled + own[64 * c : 64 * c + 64, :]

    loads[7].wait()
    chunk = 256
    rows_src = lax.broadcasted_iota(jnp.int32, (chunk, elems), 0)

    def gather(f, carry):
        ids = nbr_ref[pl.ds(f, 1), :]
        g = f + 1 - 2 * lax.rem(f, 2)
        both = jnp.zeros((160, elems), F32)
        for k in range(elems // chunk):
            hot = one_hot(rows_src == ids - k * chunk)
            both += dot(tr_ref[g, :, k * chunk : (k + 1) * chunk], hot)
        part_ref[f] = both[:80] + both[80:]
        return carry

    lax.fori_loop(0, 6, gather, 0)

    def put_partner(face, value):
        hi, lo = split2(value)
        for base, part in ((0, hi), (512, lo), (1024, hi)):
            ps_ref[base + 80 * face : base + 80 * face + 80, :] = part

    put_partner(2, part_ref[2])
    put_partner(3, part_ref[3])
    for base in (480, 992, 1504):
        ps_ref[base : base + 32, :] = jnp.zeros((32, elems), BF)

    up_x.wait()
    down_x.wait()

    @pl.when(has_high)
    def _():
        up_z.wait_send()
        down_z.wait_recv()

    @pl.when(has_low)
    def _():
        down_z.wait_send()
        up_z.wait_recv()

    loads[10].wait()
    slot_ids = lax.broadcasted_iota(jnp.int32, (80, slots), 1)
    for i, face in enumerate((0, 1, 4, 5)):
        got = recv_ref[i]
        if i < 2:
            got = jnp.where(slot_ids < live_ref[:, i : i + 1], got, 0.0)
        both = dot_nt(jnp.concatenate(split2(got), axis=0), oh_ref[i])
        put_partner(face, part_ref[face] + (both[:80] + both[80:]))
    nbr = dot(b_ref[...], ps_ref[...])
    for c in range(5):
        out_ref[c] += nbr[64 * c : 64 * c + 64, :]

    up_b.wait()
    down_b.wait()
    sums = bsend_ref[1] + brecv_ref[0] + brecv_ref[1]
    grad_ref[...] = sums[0, :owned]


def on_device(
    sectors,
    slabs,
    adjoint,
    velocity,
    drag,
    block_weight,
    flux_jac,
    face_own,
    face_nbr,
    nbr_local,
    sector_slots,
    axial_slots,
    sector_live,
    elem_block,
):
    elems = adjoint.shape[2]
    slots = sector_slots.shape[1]
    owned = BLOCKS // (sectors * slabs)
    width = -(-owned // 128) * 128
    operands = (
        adjoint,
        velocity,
        drag.reshape(1, elems),
        block_weight.reshape(1, elems),
        jnp.transpose(flux_jac, (1, 0, 2)),
        jnp.transpose(face_own, (1, 0, 2)),
        jnp.transpose(face_nbr, (1, 0, 2)),
        nbr_local,
        sector_slots,
        axial_slots,
        sector_live.reshape(1, 2),
        elem_block.reshape(1, elems),
        *constant_tables(),
    )
    vmem = pl.BlockSpec(memory_space=pltpu.VMEM)
    hbm = pl.BlockSpec(memory_space=pltpu.HBM)
    out, grad = pl.pallas_call(
        functools.partial(kernel, sectors, slabs, owned),
        out_shape=(
            pltpu.VMEM(adjoint.shape, F32),
            pltpu.VMEM((owned,), F32),
        ),
        in_specs=[hbm] * INPUTS,
        out_specs=(vmem, vmem),
        scratch_shapes=[pltpu.VMEM(a.shape, a.dtype) for a in operands]
        + [
            pltpu.VMEM((1152, elems), BF),
            pltpu.VMEM((6, 160, elems), BF),
            pltpu.VMEM((4, elems, slots), BF),
            pltpu.VMEM((4, 80, slots), F32),
            pltpu.VMEM((4, 80, slots), F32),
            pltpu.VMEM((6, 80, elems), F32),
            pltpu.VMEM((1536, elems), BF),
            pltpu.VMEM((320, 1152), BF),
            pltpu.VMEM((320, 1536), BF),
            pltpu.VMEM((3, 8, width), F32),
            pltpu.VMEM((2, 8, width), F32),
            pltpu.SemaphoreType.DMA((6,)),
            pltpu.SemaphoreType.DMA((6,)),
            pltpu.SemaphoreType.DMA((INPUTS + 5,)),
        ],
        compiler_params=pltpu.CompilerParams(
            collective_id=0, has_side_effects=True, vmem_limit_bytes=60 * 1024 * 1024
        ),
    )(*operands)
    return out, grad


def solution(mesh):
    placed = (
        P(None, None, ("sector", "axial")),
        P(None, None, ("sector", "axial")),
        P(("sector", "axial")),
        P(("sector", "axial")),
        P(),
        P(),
        P(),
        P(None, ("sector", "axial")),
        P(None, ("sector", "axial")),
        P(None, ("sector", "axial")),
        P("sector", "axial", None),
        P(("sector", "axial")),
    )
    return jax.shard_map(
        functools.partial(on_device, mesh.shape["sector"], mesh.shape["axial"]),
        mesh=mesh,
        in_specs=placed,
        out_specs=(P(None, None, ("sector", "axial")), P(("sector", "axial"))),
        check_vma=False,
    )
```
